256 devices in a mesh: dp: 32 (over z, x), tensor: 8 (over y, core).
Axes of the slice: x: 4, y: 4, z: 8, core: 2. Of those that a mesh axis runs over, the one named last changes fastest.
Arguments:
- activations: bfloat16 [28672, 4096], P('dp', 'tensor'), may hold values from -6 to 6
- out_grads: bfloat16 [28672, 4096], P('dp', 'tensor'), may hold values from -6 to 6
- gate_act: bfloat16 [28672, 14336], P('dp', 'tensor'), may hold values from -6 to 6
- w_down: bfloat16 [14336, 4096], P('tensor', 'dp'), may hold values from -0.09375 to 0.09375
- proj_in: bfloat16 [4096, 64], P('tensor'), may hold values from -0.09375 to 0.09375
- proj_out: bfloat16 [14336, 64], P('tensor'), may hold values from -0.046875 to 0.046875
- lengths: int32 [32, 8], P('dp'), may hold values from 1 to 448, 896 in all within a row
- assign: int32 [256], replicated, may hold values from 0 to 255, each once
Outputs:
- loggrads: float32 [256, 64, 64], P('dp', 'tensor')
The draws below stay inside these ranges and needn't reach their ends.
Inputs may be any that keep to these rules, and one draw needn't show every extreme that they name: `lengths`: each row gives the token counts of the 8 sequences packed into one data group's 896 rows and sums to 896. `assign`: a permutation of the sequence numbers.
All inputs are finite; a program needn't handle non-finite values.
Results may differ from the reference program's by a relative error of at most 0.013.
Values may be sent and summed in bfloat16 or wider, within the bound.
No kernel may reach another device: no remote copies, remote signals or barrier semaphores. Data moves between devices by JAX's collectives and lax.ppermute only.
A program may use at most 128 MiB of HBM per device.

```python
import math
import jax
import jax.numpy as jnp
import numpy as np
from jax import lax

D = 4096
FF = 14336
RANK = 64
TOK_DEV = 896
SEQ_GRP = 8
GROUPS = 32
SEQS = 256
TOKENS = 28672


def block_levels(stream_key, extent, pieces, low, high):
    level, own = 1.0, jax.random.fold_in(stream_key, 6)
    for dim, blocks in pieces:
        steps = jnp.exp(jax.random.uniform(jax.random.fold_in(own, dim), (blocks,), jnp.float32, low / len(pieces), high / len(pieces)))
        level = level * jnp.repeat(steps, extent[dim] // blocks).reshape([-1 if axis == dim else 1 for axis in range(len(extent))])
    return level


def split_up(count, total, limit, lean):
    portions = [(1 << 20) // math.isqrt(standing ** lean) + 1 for standing in range(2, count + 1)]
    rest, given = total - limit - (count - 1), [1] * (count - 1)
    while rest > 0:
        free = [i for i in range(count - 1) if given[i] < limit]
        whole, budget = sum([portions[i] for i in free]), rest
        for i in free:
            addition = min(limit - given[i], max(1, budget * portions[i] // whole), rest)
            given[i] = given[i] + addition
            rest = rest - addition
    return np.array([limit] + given)


def ragged_sizes(key, amount, total, bound, skew):
    if amount == 2:
        one = jax.random.randint(key, (), max(1, total - bound), min(bound, total - 1) + 1)
        return jnp.stack([one, total - one])
    sizes = jnp.asarray(split_up(amount, total, bound, skew), jnp.int32)
    pairs = (amount - 1) // 2
    source_of, taker = sizes[1:1 + 2 * pairs:2], sizes[2:2 + 2 * pairs:2]
    slack = jnp.minimum(source_of - 1, bound - taker)
    moved = jax.random.randint(jax.random.fold_in(key, 1), (pairs,), 0, 1 << 20) % (slack + 1)
    sizes = sizes.at[1:1 + 2 * pairs:2].set(source_of - moved).at[2:2 + 2 * pairs:2].set(taker + moved)
    return sizes[jax.random.permutation(jax.random.fold_in(key, 2), amount)]


def scatter_about(stream_key, extent, scale, limit, cuts=(), held_as=jnp.bfloat16):
    result = scale * jax.random.normal(stream_key, extent, jnp.float32)
    if cuts:
        result = result * block_levels(stream_key, extent, cuts, -0.22, 0.18)
    return jnp.clip(result, -limit, limit).astype(held_as)


def setup_inputs(seed: int = 0) -> dict:
    key_of = jax.random.split(jax.random.key(seed), 9)
    return {
        "activations": scatter_about(key_of[0], (TOKENS, D), 1.0, 6.0, ((0, 32), (1, 8))),
        "out_grads": scatter_about(key_of[1], (TOKENS, D), 1.0, 6.0, ((0, 32), (1, 8))),
        "gate_act": scatter_about(key_of[2], (TOKENS, FF), 1.0, 6.0, ((0, 32), (1, 8))),
        "w_down": scatter_about(key_of[3], (FF, D), D ** -0.5, 0.09375, ((0, 8), (1, 32))),
        "proj_in": scatter_about(key_of[4], (D, RANK), D ** -0.5, 0.09375, ((0, 8),)),
        "proj_out": scatter_about(key_of[5], (FF, RANK), FF ** -0.5, 0.046875, ((0, 8),)),
        "lengths": jax.vmap(lambda own: ragged_sizes(own, SEQ_GRP, TOK_DEV, TOK_DEV // 2, 2))(jax.random.split(key_of[6], GROUPS)).reshape((GROUPS, SEQ_GRP)).astype(jnp.int32),
        "assign": jax.random.permutation(key_of[7], SEQS).astype(jnp.int32),
    }


def group_grads(items):
    activations, out_grads, gate_act, seq_lengths, w_down, proj_in, proj_out = items
    in_proj = jnp.dot(activations, proj_in, preferred_element_type=jnp.float32)
    hidden_grad = jnp.dot(out_grads, w_down.T, preferred_element_type=jnp.float32)
    up_grad = (hidden_grad * gate_act.astype(jnp.float32)).astype(jnp.bfloat16)
    out_proj = jnp.dot(up_grad, proj_out, preferred_element_type=jnp.float32)
    seq_ends = jnp.cumsum(seq_lengths).astype(jnp.int32)
    starts = seq_ends - seq_lengths
    positions = lax.iota(jnp.int32, activations.shape[0])
    inside = (positions[None, :] >= starts[:, None]) & (positions[None, :] < seq_ends[:, None])
    member = jnp.where(inside, 1.0 / seq_lengths[:, None].astype(jnp.float32), 0.0).astype(jnp.float32)
    weighted = member[:, :, None] * in_proj[None, :, :]
    return jnp.einsum("ctp,tq->cpq", weighted, out_proj, precision=lax.Precision.HIGHEST)


def reference(activations, out_grads, gate_act, w_down, proj_in, proj_out, lengths, assign):
    stacked_in = activations.reshape(GROUPS, TOK_DEV, D)
    stacked_grad = out_grads.reshape(GROUPS, TOK_DEV, D)
    stacked_gate = gate_act.reshape(GROUPS, TOK_DEV, FF)

    def one_group(items):
        return group_grads((items[0], items[1], items[2], items[3], w_down, proj_in, proj_out))

    results = lax.map(one_group, (stacked_in, stacked_grad, stacked_gate, lengths))
    results = results.reshape(SEQS, RANK, RANK)
    loggrads = jnp.zeros((SEQS, RANK, RANK), jnp.float32).at[assign].set(results)
    return loggrads
```

```python
import jax
import jax.numpy as jnp
from jax import lax
from jax.sharding import PartitionSpec as P


def member_of(seq_lengths, tok_rows):
    slots = seq_lengths.shape[0]
    before = lax.iota(jnp.int32, slots)[None, :] < lax.iota(jnp.int32, slots)[:, None]
    starts = jnp.sum(jnp.where(before, seq_lengths[None, :], 0), axis=1)
    ends = starts + seq_lengths
    positions = lax.iota(jnp.int32, tok_rows)
    inside = (positions[None, :] >= starts[:, None]) & (positions[None, :] < ends[:, None])
    return jnp.where(inside, 1.0 / seq_lengths[:, None].astype(jnp.float32), 0.0)


def place(result, assign):
    slots, values = result.shape
    groups = lax.axis_size("dp")
    mine = lax.dynamic_slice_in_dim(assign, lax.axis_index("dp") * slots, slots, 0)
    placing = (mine[None, :] == lax.iota(jnp.int32, slots * groups)[:, None]).astype(jnp.bfloat16)
    spread = jnp.dot(placing, result, preferred_element_type=jnp.float32).astype(jnp.bfloat16)
    got = lax.all_to_all(spread, "dp", split_axis=0, concat_axis=0, tiled=True)
    return jnp.sum(got.reshape(groups, slots, values).astype(jnp.float32), axis=0)


def shards(activations, out_grads, gate_act, w_down, proj_in, proj_out, lengths, assign):
    tok_rows = activations.shape[0]
    rank_all = proj_in.shape[1]
    shard_count = lax.axis_size("tensor")
    slots = lengths.shape[1]
    cols = rank_all // shard_count

    in_part = jnp.dot(activations, proj_in, preferred_element_type=jnp.float32)
    in_high = in_part.astype(jnp.bfloat16)
    in_low = (in_part - in_high.astype(jnp.float32)).astype(jnp.bfloat16)
    full_grads = lax.all_gather(out_grads, "tensor", axis=1, tiled=True)
    in_all = lax.all_gather(jnp.concatenate([in_high, in_low], axis=1), "tensor", axis=0)
    in_all = jnp.sum(in_all.astype(jnp.float32), axis=0)
    in_sum = in_all[:, :rank_all] + in_all[:, rank_all:]
    weighted = member_of(lengths[0], tok_rows)[:, :, None] * in_sum[None, :, :]

    hidden_grad = lax.dot_general(
        full_grads,
        lax.all_gather(w_down, "dp", axis=1, tiled=True),
        (((1,), (1,)), ((), ())),
        preferred_element_type=jnp.float32,
    )
    up_grad = (hidden_grad * gate_act.astype(jnp.float32)).astype(jnp.bfloat16)
    out_part = jnp.dot(up_grad, proj_out, preferred_element_type=jnp.float32)
    part = jnp.einsum("ctp,tq->cpq", weighted, out_part, precision=lax.Precision.HIGHEST)
    part = part.reshape(slots, shard_count, cols * rank_all).transpose(1, 0, 2)
    result = jnp.sum(lax.all_to_all(part, "tensor", split_axis=0, concat_axis=0, tiled=True), axis=0)
    return place(result.astype(jnp.bfloat16), assign).reshape(slots, cols, rank_all)


def solution(mesh):
    in_specs = (
        P("dp", "tensor"),
        P("dp", "tensor"),
        P("dp", "tensor"),
        P("tensor", "dp"),
        P("tensor", None),
        P("tensor", None),
        P("dp", None),
        P(),
    )
    out_specs = P("dp", "tensor", None)
    return jax.shard_map(shards, mesh=mesh, in_specs=in_specs, out_specs=out_specs, check_vma=False)
```

```python
import functools

import jax
import jax.numpy as jnp
from jax import lax
from jax.experimental import pallas as pl
from jax.experimental.layout import Layout, with_layout_constraint
from jax.experimental.pallas import tpu as pltpu
from jax.sharding import PartitionSpec as P

NZ, NX, NY, NC = 8, 4, 4, 2
TILE = 384
DISTANCES = (0, -1, 1, -2, 2, -3, 3, 4)
PARTS = 4
VMEM = 58 * 2**20
FIRST = 768


def move(array, axis, dist):
    if axis == "z":
        pairs = [(z * NX + x, (z + dist) % NZ * NX + x) for z in range(NZ) for x in range(NX)]
        return lax.ppermute(array, "dp", pairs)
    if axis == "x":
        pairs = [(z * NX + x, z * NX + (x + dist) % NX) for z in range(NZ) for x in range(NX)]
        return lax.ppermute(array, "dp", pairs)
    if axis == "y":
        pairs = [(y * NC + c, (y + dist) % NY * NC + c) for y in range(NY) for c in range(NC)]
        return lax.ppermute(array, "tensor", pairs)
    pairs = [(y * NC + c, y * NC + (c + dist) % NC) for y in range(NY) for c in range(NC)]
    return lax.ppermute(array, "tensor", pairs)


class Blocks:
    def __init__(self, array, stretches):
        self.array, self.stretches = array, stretches

    def sent(self, axis, dist, name):
        dz, dx = (dist, 0) if axis == "z" else (0, dist)
        with jax.named_scope(name):
            array = move(self.array, axis, dist)
        return Blocks(array, [(z - dz, x - dx, r, n) for z, x, r, n in self.stretches])

    def part(self, begin, end):
        kept, at = [], 0
        for z, x, r, n in self.stretches:
            low, high = max(begin, at), min(end, at + n)
            if low < high:
                kept.append((z, x, r + low - at, high - low))
            at += n
        return Blocks(self.array[begin:end], kept)

    def halves(self):
        rows = self.array.shape[0]
        middle = rows // 32 * 16
        return self.part(0, middle), self.part(middle, rows)

    def after(self, *others):
        return Blocks(after(self.array, *[o.array for o in others]), self.stretches)


def after(array, *others):
    return lax.optimization_barrier((array, *others))[0]


def joined(blocks):
    return Blocks(
        jnp.concatenate([b.array for b in blocks], axis=0), [s for b in blocks for s in b.stretches]
    )


def ring(block, axis, size, name, waits={}):
    up, down, got = block, block, []
    for step in range(1, size // 2):
        if step in waits:
            up, down = up.after(*waits[step]), down.after(*waits[step])
        up, down = up.sent(axis, 1, f"{name}_up{step}"), down.sent(axis, -1, f"{name}_down{step}")
        got.append((up, down))
    last = up.halves()[0].sent(axis, 1, f"{name}_up_last"), down.halves()[1].sent(axis, -1, f"{name}_down_last")
    return got, last


def ring_of_pair(one, two, axis, size, name):
    up, down, got = (one, two), (one, two), []
    for step in range(1, size // 2):
        up_one = up[0].sent(axis, 1, f"{name}_up{step}_one")
        down_two = down[1].sent(axis, -1, f"{name}_down{step}_two")
        up_two = up[1].sent(axis, 1, f"{name}_up{step}_two")
        down_one = down[0].sent(axis, -1, f"{name}_down{step}_one")
        up, down = (up_one, up_two), (down_one, down_two)
        got += [up_one, down_two, up_two, down_one]
    return got, [up[0].sent(axis, 1, f"{name}_up_last"), down[1].sent(axis, -1, f"{name}_down_last")]


def project_kernel(stretches, start, place_ref, full_ref, gate_ref, proj_ref, *refs):
    block_refs = refs[: len(stretches)]
    out_ref, grads, weights, gate, total, sem = refs[len(stretches) :]
    shards, k, toks = grads.shape
    rows = weights.shape[1]
    z, x = place_ref[0], place_ref[1]
    per = NZ // PARTS
    copies, parts = [], [[] for _ in range(PARTS)]

    def copy(part, source, target):
        each = pltpu.make_async_copy(source, target, sem.at[len(copies)])
        copies.append(each)
        parts[part].append(each)

    for part in range(PARTS):
        for at in range(part * per, (part + 1) * per):
            copy(part, full_ref.at[lax.rem(z + NZ + DISTANCES[at], NZ), pl.ds(0, k), :], grads.at[at])
        for ref, spans in zip(block_refs, stretches):
            begin = 0
            for dz, dx, row, n in spans:
                at = DISTANCES.index(dz if dz in DISTANCES else dz % NZ)
                if at // per == part:
                    slot = at * NX + lax.rem(x + 2 * NX + dx, NX)
                    copy(part, ref.at[pl.ds(begin, n), :], weights.at[slot, pl.ds(row, n), :])
                begin += n
    copy(PARTS - 1, gate_ref.at[pl.ds(start, rows), :], gate)
    for each in copies:
        each.start()
    out_ref[...] = jnp.zeros_like(out_ref)

    def tile_of(part, at, size):
        tile = pl.ds(at, size)
        hidden = jnp.dot(
            jnp.concatenate([weights[i, tile, :] for i in range(part * per * NX, (part + 1) * per * NX)], axis=1),
            jnp.concatenate([grads[i] for i in range(part * per, (part + 1) * per)], axis=0),
            preferred_element_type=jnp.float32,
        )
        if part:
            hidden += total[tile, :]
        if part < PARTS - 1:
            total[tile, :] = hidden
            return
        up_grad = (hidden * gate[tile, :].astype(jnp.float32)).astype(jnp.bfloat16)
        out_ref[...] += jnp.dot(
            proj_ref[:, pl.ds(start + at, size)], up_grad, preferred_element_type=jnp.float32
        )

    for part in range(PARTS):
        for each in parts[part]:
            each.wait()
        for at in range(0, rows, TILE):
            tile_of(part, at, min(TILE, rows - at))


def project(blocks, full, start, rows, place, gate_t, proj_t):
    toks, rank = gate_t.shape[1], proj_t.shape[0]
    stretches = [b.stretches for b in blocks]
    shards, devices = full.shape[0], NZ * NX
    features = 128 * devices
    n_copies = sum(len(s) for s in stretches) + shards + 1
    any_ref = pl.BlockSpec(memory_space=pl.ANY)
    return pl.pallas_call(
        functools.partial(project_kernel, stretches, start),
        out_shape=jax.ShapeDtypeStruct((rank, toks), jnp.float32),
        in_specs=[pl.BlockSpec(memory_space=pltpu.SMEM), any_ref, any_ref, pl.BlockSpec(memory_space=pltpu.VMEM)]
        + [any_ref] * len(blocks),
        out_specs=pl.BlockSpec(memory_space=pltpu.VMEM),
        scratch_shapes=[
            pltpu.VMEM((shards, features // shards, toks), jnp.bfloat16),
            pltpu.VMEM((devices, rows, 128), jnp.bfloat16),
            pltpu.VMEM((rows, toks), jnp.bfloat16),
            pltpu.VMEM((rows, toks), jnp.float32),
            pltpu.SemaphoreType.DMA((n_copies,)),
        ],
        compiler_params=pltpu.CompilerParams(vmem_limit_bytes=VMEM),
        cost_estimate=pl.CostEstimate(
            flops=2 * toks * rows * (features + 256),
            bytes_accessed=2 * (features * (toks + rows) + toks * rows),
            transcendentals=0,
        ),
    )(place, full, gate_t, proj_t, *[b.array for b in blocks])


def member_of(seq_lengths, tok_rows):
    slots = seq_lengths.shape[0]
    before = lax.iota(jnp.int32, slots)[None, :] < lax.iota(jnp.int32, slots)[:, None]
    starts = jnp.sum(jnp.where(before, seq_lengths[None, :], 0), axis=1)
    ends = starts + seq_lengths
    positions = lax.iota(jnp.int32, tok_rows)
    inside = (positions[None, :] >= starts[:, None]) & (positions[None, :] < ends[:, None])
    return jnp.where(inside, 1.0 / seq_lengths[:, None].astype(jnp.float32), 0.0)


def hand_over(result, assign):
    slots, values = result.shape
    groups = lax.axis_size("dp")
    mine = lax.dynamic_slice_in_dim(assign, lax.axis_index("dp") * slots, slots, 0)
    placing = (mine[None, :] == lax.iota(jnp.int32, slots * groups)[:, None]).astype(jnp.bfloat16)
    spread = jnp.dot(placing, result, preferred_element_type=jnp.float32).astype(jnp.bfloat16)
    got = lax.all_to_all(spread, "dp", split_axis=0, concat_axis=0, tiled=True)
    return jnp.sum(got.reshape(groups, slots, values).astype(jnp.float32), axis=0)


def shards(activations, out_grads, gate_act, w_down, proj_in, proj_out, lengths, assign):
    tok_rows, feat = out_grads.shape
    rank_all = proj_in.shape[1]
    shard_count = lax.axis_size("tensor")
    slots = lengths.shape[1]
    cols = rank_all // shard_count
    group, shard = lax.axis_index("dp"), lax.axis_index("tensor")
    place = jnp.stack([group // NX, group % NX, shard // NC, shard % NC]).astype(jnp.int32)

    in_part = jnp.dot(activations, proj_in, preferred_element_type=jnp.float32)
    in_high = in_part.astype(jnp.bfloat16)
    in_low = (in_part - in_high.astype(jnp.float32)).astype(jnp.bfloat16)
    own = jnp.concatenate([out_grads.T, in_high.T, in_low.T], axis=0)
    own = with_layout_constraint(own, Layout(major_to_minor=(0, 1)))

    rows = w_down.shape[0]
    first = Blocks(w_down[:FIRST], [(0, 0, 0, FIRST)])
    other = Blocks(w_down[FIRST:], [(0, 0, 0, rows - FIRST)])
    first_up, first_down = first.sent("x", 1, "first_x_up"), first.sent("x", -1, "first_x_down")
    first_far = first.sent("x", 2, "first_x_far")
    other_z, other_z_last = ring(other, "z", NZ, "other_z")
    near = joined([other, *other_z[0], other_z[1][0]])
    far = joined([other_z[1][1], *other_z[2], *other_z_last])
    near = near.after(first_up, first_down, first_far)
    far = far.after(first_up, first_down, first_far)
    other_x, other_x_last = ring_of_pair(near, far, "x", NX, "other_x")
    first_x = joined([first, first_up, first_down, first_far]).after(far)
    first_z, first_z_last = ring(first_x, "z", NZ, "first_z", {2: other_x[:2], 3: other_x[2:]})

    full = lax.all_gather(own, "tensor", axis=0)
    full = with_layout_constraint(full, Layout(major_to_minor=(0, 1, 2)))
    in_all = jnp.sum(full[:, feat:].astype(jnp.float32), axis=0)
    in_sum = in_all[:rank_all] + in_all[rank_all:]
    weighted = member_of(lengths[0], tok_rows)[:, None, :] * in_sum[None, :, :]

    proj_t, gate_t = proj_out.T, after(gate_act, other_z_last[0].array).T
    first_all = [first_x, *[b for pair in first_z for b in pair], *first_z_last]
    out_part = project(first_all, full, 0, FIRST, place, gate_t, proj_t)
    other_all = [near, far, *other_x, *other_x_last]
    out_part += project(other_all, full, FIRST, rows - FIRST, place, gate_t, proj_t)

    part = jnp.einsum("cpt,qt->cpq", weighted, out_part, precision=lax.Precision.HIGHEST)
    part = part.reshape(slots, shard_count, cols * rank_all).transpose(1, 0, 2)
    result = jnp.sum(lax.all_to_all(part, "tensor", split_axis=0, concat_axis=0, tiled=True), axis=0)
    return hand_over(result.astype(jnp.bfloat16), assign).reshape(slots, cols, rank_all)


def solution(mesh):
    in_specs = (
        P("dp", "tensor"),
        P("dp", "tensor"),
        P("dp", "tensor"),
        P("tensor", "dp"),
        P("tensor", None),
        P("tensor", None),
        P("dp", None),
        P(),
    )
    out_specs = P("dp", "tensor", None)
    return jax.shard_map(shards, mesh=mesh, in_specs=in_specs, out_specs=out_specs, check_vma=False)
```

```python
import functools

import jax
import jax.numpy as jnp
from jax import lax
from jax.experimental import pallas as pl
from jax.experimental.layout import Layout, with_layout_constraint
from jax.experimental.pallas import tpu as pltpu
from jax.sharding import PartitionSpec as P

NZ, NX, NY, NC = 8, 4, 4, 2
TILE = 512
DISTANCES = (0, -1, 1, -2, 2, -3, 3, 4)
PARTS = 4
VMEM = 58 * 2**20
FIRST = 896


def move(array, axis, dist):
    if axis == "z":
        pairs = [(z * NX + x, (z + dist) % NZ * NX + x) for z in range(NZ) for x in range(NX)]
        return lax.ppermute(array, "dp", pairs)
    if axis == "x":
        pairs = [(z * NX + x, z * NX + (x + dist) % NX) for z in range(NZ) for x in range(NX)]
        return lax.ppermute(array, "dp", pairs)
    if axis == "y":
        pairs = [(y * NC + c, (y + dist) % NY * NC + c) for y in range(NY) for c in range(NC)]
        return lax.ppermute(array, "tensor", pairs)
    pairs = [(y * NC + c, y * NC + (c + dist) % NC) for y in range(NY) for c in range(NC)]
    return lax.ppermute(array, "tensor", pairs)


class Blocks:
    def __init__(self, array, stretches):
        self.array, self.stretches = array, stretches

    def sent(self, axis, dist, name):
        dz, dx = (dist, 0) if axis == "z" else (0, dist)
        with jax.named_scope(name):
            array = move(self.array, axis, dist)
        return Blocks(array, [(z - dz, x - dx, r, n) for z, x, r, n in self.stretches])

    def part(self, begin, end):
        kept, at = [], 0
        for z, x, r, n in self.stretches:
            low, high = max(begin, at), min(end, at + n)
            if low < high:
                kept.append((z, x, r + low - at, high - low))
            at += n
        return Blocks(self.array[begin:end], kept)

    def halves(self):
        rows = self.array.shape[0]
        middle = rows // 32 * 16
        return self.part(0, middle), self.part(middle, rows)

    def after(self, *others):
        return Blocks(after(self.array, *[o.array for o in others]), self.stretches)


def after(array, *others):
    return lax.optimization_barrier((array, *others))[0]


def joined(blocks):
    return Blocks(
        jnp.concatenate([b.array for b in blocks], axis=0), [s for b in blocks for s in b.stretches]
    )


def ring(block, axis, size, name, waits={}):
    up, down, got = block, block, []
    for step in range(1, size // 2):
        if step in waits:
            up, down = up.after(*waits[step]), down.after(*waits[step])
        up, down = up.sent(axis, 1, f"{name}_up{step}"), down.sent(axis, -1, f"{name}_down{step}")
        got.append((up, down))
    last = up.halves()[0].sent(axis, 1, f"{name}_up_last"), down.halves()[1].sent(axis, -1, f"{name}_down_last")
    return got, last


def ring_of_pair(one, two, axis, size, name):
    up, down, got = (one, two), (one, two), []
    for step in range(1, size // 2):
        up_one = up[0].sent(axis, 1, f"{name}_up{step}_one")
        down_two = down[1].sent(axis, -1, f"{name}_down{step}_two")
        up_two = up[1].sent(axis, 1, f"{name}_up{step}_two")
        down_one = down[0].sent(axis, -1, f"{name}_down{step}_one")
        up, down = (up_one, up_two), (down_one, down_two)
        got += [up_one, down_two, up_two, down_one]
    return got, [up[0].sent(axis, 1, f"{name}_up_last"), down[1].sent(axis, -1, f"{name}_down_last")]


def project_kernel(stretches, start, place_ref, full_ref, gate_ref, proj_ref, *refs):
    block_refs = refs[: len(stretches)]
    out_ref, grads, weights, gate, total, sem = refs[len(stretches) :]
    shards, k, toks = grads.shape
    rows = weights.shape[1]
    z, x = place_ref[0], place_ref[1]
    per = NZ // PARTS
    copies, parts = [], [[] for _ in range(PARTS)]

    def copy(part, source, target):
        each = pltpu.make_async_copy(source, target, sem.at[len(copies)])
        copies.append(each)
        parts[part].append(each)

    for part in range(PARTS):
        for at in range(part * per, (part + 1) * per):
            copy(part, full_ref.at[lax.rem(z + NZ + DISTANCES[at], NZ), pl.ds(0, k), :], grads.at[at])
        for ref, spans in zip(block_refs, stretches):
            begin = 0
            for dz, dx, row, n in spans:
                at = DISTANCES.index(dz if dz in DISTANCES else dz % NZ)
                if at // per == part:
                    slot = at * NX + lax.rem(x + 2 * NX + dx, NX)
                    copy(part, ref.at[pl.ds(begin, n), :], weights.at[slot, pl.ds(row, n), :])
                begin += n
    copy(PARTS - 1, gate_ref.at[pl.ds(start, rows), :], gate)
    for each in copies:
        each.start()
    out_ref[...] = jnp.zeros_like(out_ref)

    def tile_of(part, at, size):
        tile = pl.ds(at, size)
        hidden = jnp.dot(
            jnp.concatenate([weights[i, tile, :] for i in range(part * per * NX, (part + 1) * per * NX)], axis=1),
            jnp.concatenate([grads[i] for i in range(part * per, (part + 1) * per)], axis=0),
            preferred_element_type=jnp.float32,
        )
        if part:
            hidden += total[tile, :]
        if part < PARTS - 1:
            total[tile, :] = hidden
            return
        up_grad = (hidden * gate[tile, :].astype(jnp.float32)).astype(jnp.bfloat16)
        out_ref[...] += jnp.dot(
            proj_ref[:, pl.ds(start + at, size)], up_grad, preferred_element_type=jnp.float32
        )

    for part in range(PARTS):
        for each in parts[part]:
            each.wait()
        for at in range(0, rows, TILE):
            tile_of(part, at, min(TILE, rows - at))


def project(blocks, full, start, rows, place, gate_t, proj_t):
    toks, rank = gate_t.shape[1], proj_t.shape[0]
    stretches = [b.stretches for b in blocks]
    shards, devices = full.shape[0], NZ * NX
    features = 128 * devices
    n_copies = sum(len(s) for s in stretches) + shards + 1
    any_ref = pl.BlockSpec(memory_space=pl.ANY)
    return pl.pallas_call(
        functools.partial(project_kernel, stretches, start),
        out_shape=jax.ShapeDtypeStruct((rank, toks), jnp.float32),
        in_specs=[pl.BlockSpec(memory_space=pltpu.SMEM), any_ref, any_ref, pl.BlockSpec(memory_space=pltpu.VMEM)]
        + [any_ref] * len(blocks),
        out_specs=pl.BlockSpec(memory_space=pltpu.VMEM),
        scratch_shapes=[
            pltpu.VMEM((shards, features // shards, toks), jnp.bfloat16),
            pltpu.VMEM((devices, rows, 128), jnp.bfloat16),
            pltpu.VMEM((rows, toks), jnp.bfloat16),
            pltpu.VMEM((rows, toks), jnp.float32),
            pltpu.SemaphoreType.DMA((n_copies,)),
        ],
        compiler_params=pltpu.CompilerParams(vmem_limit_bytes=VMEM),
        cost_estimate=pl.CostEstimate(
            flops=2 * toks * rows * (features + 256),
            bytes_accessed=2 * (features * (toks + rows) + toks * rows),
            transcendentals=0,
        ),
    )(place, full, gate_t, proj_t, *[b.array for b in blocks])


def member_of(seq_lengths, tok_rows):
    slots = seq_lengths.shape[0]
    before = lax.iota(jnp.int32, slots)[None, :] < lax.iota(jnp.int32, slots)[:, None]
    starts = jnp.sum(jnp.where(before, seq_lengths[None, :], 0), axis=1)
    ends = starts + seq_lengths
    positions = lax.iota(jnp.int32, tok_rows)
    inside = (positions[None, :] >= starts[:, None]) & (positions[None, :] < ends[:, None])
    return jnp.where(inside, 1.0 / seq_lengths[:, None].astype(jnp.float32), 0.0)


def hand_over(result, assign):
    slots, values = result.shape
    groups = lax.axis_size("dp")
    mine = lax.dynamic_slice_in_dim(assign, lax.axis_index("dp") * slots, slots, 0)
    placing = (mine[None, :] == lax.iota(jnp.int32, slots * groups)[:, None]).astype(jnp.bfloat16)
    spread = jnp.dot(placing, result, preferred_element_type=jnp.float32).astype(jnp.bfloat16)
    got = lax.all_to_all(spread, "dp", split_axis=0, concat_axis=0, tiled=True)
    return jnp.sum(got.reshape(groups, slots, values).astype(jnp.float32), axis=0)


def shards(activations, out_grads, gate_act, w_down, proj_in, proj_out, lengths, assign):
    tok_rows, feat = out_grads.shape
    rank_all = proj_in.shape[1]
    shard_count = lax.axis_size("tensor")
    slots = lengths.shape[1]
    cols = rank_all // shard_count
    group, shard = lax.axis_index("dp"), lax.axis_index("tensor")
    place = jnp.stack([group // NX, group % NX, shard // NC, shard % NC]).astype(jnp.int32)

    in_part = jnp.dot(activations, proj_in, preferred_element_type=jnp.float32)
    in_high = in_part.astype(jnp.bfloat16)
    in_low = (in_part - in_high.astype(jnp.float32)).astype(jnp.bfloat16)
    own = jnp.concatenate([out_grads.T, in_high.T, in_low.T], axis=0)
    own = with_layout_constraint(own, Layout(major_to_minor=(0, 1)))

    rows = w_down.shape[0]
    first = Blocks(w_down[:FIRST], [(0, 0, 0, FIRST)])
    other = Blocks(w_down[FIRST:], [(0, 0, 0, rows - FIRST)])
    first_up, first_down = first.sent("x", 1, "first_x_up"), first.sent("x", -1, "first_x_down")
    first_far = first.sent("x", 2, "first_x_far")
    other_z, other_z_last = ring(other, "z", NZ, "other_z")
    near = joined([other, *other_z[0], other_z[1][0]])
    far = joined([other_z[1][1], *other_z[2], *other_z_last])
    near = near.after(first_up, first_down, first_far)
    far = far.after(first_up, first_down, first_far)
    other_x, other_x_last = ring_of_pair(near, far, "x", NX, "other_x")
    first_x = joined([first, first_up, first_down, first_far]).after(far)
    first_z, first_z_last = ring(first_x, "z", NZ, "first_z", {2: other_x[:2], 3: other_x[2:]})

    full = lax.all_gather(own, "tensor", axis=0)
    full = with_layout_constraint(full, Layout(major_to_minor=(0, 1, 2)))
    in_all = jnp.sum(full[:, feat:].astype(jnp.float32), axis=0)
    in_sum = in_all[:rank_all] + in_all[rank_all:]
    weighted = member_of(lengths[0], tok_rows)[:, None, :] * in_sum[None, :, :]

    proj_t, gate_t = proj_out.T, after(gate_act, other_z_last[0].array).T
    first_all = [first_x, *[b for pair in first_z for b in pair], *first_z_last]
    out_part = project(first_all, full, 0, FIRST, place, gate_t, proj_t)
    other_all = [near, far, *other_x, *other_x_last]
    out_part += project(other_all, full, FIRST, rows - FIRST, place, gate_t, proj_t)

    part = jnp.einsum("cpt,qt->cpq", weighted, out_part, precision=lax.Precision.HIGHEST)
    part = part.reshape(slots, shard_count, cols * rank_all).transpose(1, 0, 2)
    result = jnp.sum(lax.all_to_all(part, "tensor", split_axis=0, concat_axis=0, tiled=True), axis=0)
    return hand_over(result.astype(jnp.bfloat16), assign).reshape(slots, cols, rank_all)


def solution(mesh):
    in_specs = (
        P("dp", "tensor"),
        P("dp", "tensor"),
        P("dp", "tensor"),
        P("tensor", "dp"),
        P("tensor", None),
        P("tensor", None),
        P("dp", None),
        P(),
    )
    out_specs = P("dp", "tensor", None)
    return jax.shard_map(shards, mesh=mesh, in_specs=in_specs, out_specs=out_specs, check_vma=False)
```

```python
import functools

import jax
import jax.numpy as jnp
from jax import lax
from jax.experimental import pallas as pl
from jax.experimental.layout import Layout, with_layout_constraint
from jax.experimental.pallas import tpu as pltpu
from jax.sharding import PartitionSpec as P

NZ, NX, NY, NC = 8, 4, 4, 2
TILE = 512
DISTANCES = (0, -1, 1, -2, 2, -3, 3, 4)
PARTS = 4
VMEM = 58 * 2**20
FIRST = 896


def move(array, axis, dist):
    if axis == "z":
        pairs = [(z * NX + x, (z + dist) % NZ * NX + x) for z in range(NZ) for x in range(NX)]
        return lax.ppermute(array, "dp", pairs)
    if axis == "x":
        pairs = [(z * NX + x, z * NX + (x + dist) % NX) for z in range(NZ) for x in range(NX)]
        return lax.ppermute(array, "dp", pairs)
    if axis == "y":
        pairs = [(y * NC + c, (y + dist) % NY * NC + c) for y in range(NY) for c in range(NC)]
        return lax.ppermute(array, "tensor", pairs)
    pairs = [(y * NC + c, y * NC + (c + dist) % NC) for y in range(NY) for c in range(NC)]
    return lax.ppermute(array, "tensor", pairs)


class Blocks:
    def __init__(self, array, stretches):
        self.array, self.stretches = array, stretches

    def sent(self, axis, dist, name):
        dz, dx = (dist, 0) if axis == "z" else (0, dist)
        with jax.named_scope(name):
            array = move(self.array, axis, dist)
        return Blocks(array, [(z - dz, x - dx, r, n) for z, x, r, n in self.stretches])

    def part(self, begin, end):
        kept, at = [], 0
        for z, x, r, n in self.stretches:
            low, high = max(begin, at), min(end, at + n)
            if low < high:
                kept.append((z, x, r + low - at, high - low))
            at += n
        return Blocks(self.array[begin:end], kept)

    def halves(self):
        rows = self.array.shape[0]
        middle = rows // 32 * 16
        return self.part(0, middle), self.part(middle, rows)

    def after(self, *others):
        return Blocks(after(self.array, *[o.array for o in others]), self.stretches)


def after(array, *others):
    return lax.optimization_barrier((array, *others))[0]


def joined(blocks):
    return Blocks(
        jnp.concatenate([b.array for b in blocks], axis=0), [s for b in blocks for s in b.stretches]
    )


def ring(block, axis, size, name, waits={}):
    up, down, got = block, block, []
    for step in range(1, size // 2):
        if step in waits:
            up, down = up.after(*waits[step]), down.after(*waits[step])
        up, down = up.sent(axis, 1, f"{name}_up{step}"), down.sent(axis, -1, f"{name}_down{step}")
        got.append((up, down))
    last = up.halves()[0].sent(axis, 1, f"{name}_up_last"), down.halves()[1].sent(axis, -1, f"{name}_down_last")
    return got, last


def ring_of_pair(one, two, axis, size, name):
    up, down, got = (one, two), (one, two), []
    for step in range(1, size // 2):
        up_one = up[0].sent(axis, 1, f"{name}_up{step}_one")
        down_two = down[1].sent(axis, -1, f"{name}_down{step}_two")
        up_two = up[1].sent(axis, 1, f"{name}_up{step}_two")
        down_one = down[0].sent(axis, -1, f"{name}_down{step}_one")
        up, down = (up_one, up_two), (down_one, down_two)
        got += [up_one, down_two, up_two, down_one]
    return got, [up[0].sent(axis, 1, f"{name}_up_last"), down[1].sent(axis, -1, f"{name}_down_last")]


def project_kernel(stretches, start, place_ref, full_ref, gate_ref, proj_ref, *refs):
    block_refs = refs[: len(stretches)]
    out_ref, grads, weights, gate, total, sem = refs[len(stretches) :]
    shards, k, toks = grads.shape
    rows = weights.shape[1]
    z, x = place_ref[0], place_ref[1]
    per = NZ // PARTS
    copies, parts = [], [[] for _ in range(PARTS)]

    def copy(part, source, target):
        each = pltpu.make_async_copy(source, target, sem.at[len(copies)])
        copies.append(each)
        parts[part].append(each)

    for part in range(PARTS):
        for at in range(part * per, (part + 1) * per):
            copy(part, full_ref.at[lax.rem(z + NZ + DISTANCES[at], NZ), pl.ds(0, k), :], grads.at[at])
        for ref, spans in zip(block_refs, stretches):
            begin = 0
            for dz, dx, row, n in spans:
                at = DISTANCES.index(dz if dz in DISTANCES else dz % NZ)
                if at // per == part:
                    slot = at * NX + lax.rem(x + 2 * NX + dx, NX)
                    copy(part, ref.at[pl.ds(begin, n), :], weights.at[slot, pl.ds(row, n), :])
                begin += n
    copy(PARTS - 1, gate_ref.at[pl.ds(start, rows), :], gate)
    for each in copies:
        each.start()
    out_ref[...] = jnp.zeros_like(out_ref)

    def tile_of(part, at, size):
        tile = pl.ds(at, size)
        hidden = jnp.dot(
            jnp.concatenate([weights[i, tile, :] for i in range(part * per * NX, (part + 1) * per * NX)], axis=1),
            jnp.concatenate([grads[i] for i in range(part * per, (part + 1) * per)], axis=0),
            preferred_element_type=jnp.float32,
        )
        if part:
            hidden += total[tile, :]
        if part < PARTS - 1:
            total[tile, :] = hidden
            return
        up_grad = (hidden * gate[tile, :].astype(jnp.float32)).astype(jnp.bfloat16)
        out_ref[...] += jnp.dot(
            proj_ref[:, pl.ds(start + at, size)], up_grad, preferred_element_type=jnp.float32
        )

    for part in range(PARTS):
        for each in parts[part]:
            each.wait()
        for at in range(0, rows, TILE):
            tile_of(part, at, min(TILE, rows - at))


def project(blocks, full, start, rows, place, gate_t, proj_t):
    toks, rank = gate_t.shape[1], proj_t.shape[0]
    stretches = [b.stretches for b in blocks]
    shards, devices = full.shape[0], NZ * NX
    features = 128 * devices
    n_copies = sum(len(s) for s in stretches) + shards + 1
    any_ref = pl.BlockSpec(memory_space=pl.ANY)
    return pl.pallas_call(
        functools.partial(project_kernel, stretches, start),
        out_shape=jax.ShapeDtypeStruct((rank, toks), jnp.float32),
        in_specs=[pl.BlockSpec(memory_space=pltpu.SMEM), any_ref, any_ref, pl.BlockSpec(memory_space=pltpu.VMEM)]
        + [any_ref] * len(blocks),
        out_specs=pl.BlockSpec(memory_space=pltpu.VMEM),
        scratch_shapes=[
            pltpu.VMEM((shards, features // shards, toks), jnp.bfloat16),
            pltpu.VMEM((devices, rows, 128), jnp.bfloat16),
            pltpu.VMEM((rows, toks), jnp.bfloat16),
            pltpu.VMEM((rows, toks), jnp.float32),
            pltpu.SemaphoreType.DMA((n_copies,)),
        ],
        compiler_params=pltpu.CompilerParams(vmem_limit_bytes=VMEM),
        cost_estimate=pl.CostEstimate(
            flops=2 * toks * rows * (features + 256),
            bytes_accessed=2 * (features * (toks + rows) + toks * rows),
            transcendentals=0,
        ),
    )(place, full, gate_t, proj_t, *[b.array for b in blocks])


def member_of(seq_lengths, tok_rows):
    slots = seq_lengths.shape[0]
    before = lax.iota(jnp.int32, slots)[None, :] < lax.iota(jnp.int32, slots)[:, None]
    starts = jnp.sum(jnp.where(before, seq_lengths[None, :], 0), axis=1)
    ends = starts + seq_lengths
    positions = lax.iota(jnp.int32, tok_rows)
    inside = (positions[None, :] >= starts[:, None]) & (positions[None, :] < ends[:, None])
    return jnp.where(inside, 1.0 / seq_lengths[:, None].astype(jnp.float32), 0.0)


def hand_over(result, assign):
    slots, values = result.shape
    groups = lax.axis_size("dp")
    mine = lax.dynamic_slice_in_dim(assign, lax.axis_index("dp") * slots, slots, 0)
    placing = (mine[None, :] == lax.iota(jnp.int32, slots * groups)[:, None]).astype(jnp.bfloat16)
    spread = jnp.dot(placing, result, preferred_element_type=jnp.float32).astype(jnp.bfloat16)
    got = lax.all_to_all(spread, "dp", split_axis=0, concat_axis=0, tiled=True)
    return jnp.sum(got.reshape(groups, slots, values).astype(jnp.float32), axis=0)


def shards(activations, out_grads, gate_act, w_down, proj_in, proj_out, lengths, assign):
    tok_rows, feat = out_grads.shape
    rank_all = proj_in.shape[1]
    shard_count = lax.axis_size("tensor")
    slots = lengths.shape[1]
    cols = rank_all // shard_count
    group, shard = lax.axis_index("dp"), lax.axis_index("tensor")
    place = jnp.stack([group // NX, group % NX, shard // NC, shard % NC]).astype(jnp.int32)

    rows = w_down.shape[0]
    first = Blocks(w_down[:FIRST], [(0, 0, 0, FIRST)])
    other = Blocks(w_down[FIRST:], [(0, 0, 0, rows - FIRST)])
    first_up, first_down = first.sent("x", 1, "first_x_up"), first.sent("x", -1, "first_x_down")
    first_far = first.sent("x", 2, "first_x_far")
    other_z, other_z_last = ring(other, "z", NZ, "other_z")
    activations, out_grads = (after(a, *[b.array for b in (*other_z[0], first_up, first_down, first_far)]) for a in (activations, out_grads))
    in_part = jnp.dot(activations, proj_in, preferred_element_type=jnp.float32)
    in_high = in_part.astype(jnp.bfloat16)
    in_low = (in_part - in_high.astype(jnp.float32)).astype(jnp.bfloat16)
    own = jnp.concatenate([out_grads.T, in_high.T, in_low.T], axis=0)
    own = with_layout_constraint(own, Layout(major_to_minor=(0, 1)))

    near = joined([other, *other_z[0], other_z[1][0]])
    far = joined([other_z[1][1], *other_z[2], *other_z_last])
    near = near.after(first_up, first_down, first_far)
    far = far.after(first_up, first_down, first_far)
    other_x, other_x_last = ring_of_pair(near, far, "x", NX, "other_x")
    first_x = joined([first, first_up, first_down, first_far]).after(far)
    first_z, first_z_last = ring(first_x, "z", NZ, "first_z", {2: other_x[:2], 3: other_x[2:]})

    full = lax.all_gather(own, "tensor", axis=0)
    full = with_layout_constraint(full, Layout(major_to_minor=(0, 1, 2)))
    in_all = jnp.sum(full[:, feat:].astype(jnp.float32), axis=0)
    in_sum = in_all[:rank_all] + in_all[rank_all:]
    weighted = member_of(lengths[0], tok_rows)[:, None, :] * in_sum[None, :, :]

    proj_t, gate_t = proj_out.T, after(gate_act, other_z_last[0].array).T
    first_all = [first_x, *[b for pair in first_z for b in pair], *first_z_last]
    out_part = project(first_all, full, 0, FIRST, place, gate_t, proj_t)
    other_all = [near, far, *other_x, *other_x_last]
    out_part += project(other_all, full, FIRST, rows - FIRST, place, gate_t, proj_t)

    part = jnp.einsum("cpt,qt->cpq", weighted, out_part, precision=lax.Precision.HIGHEST)
    part = part.reshape(slots, shard_count, cols * rank_all).transpose(1, 0, 2)
    result = jnp.sum(lax.all_to_all(part, "tensor", split_axis=0, concat_axis=0, tiled=True), axis=0)
    return hand_over(result.astype(jnp.bfloat16), assign).reshape(slots, cols, rank_all)


def solution(mesh):
    in_specs = (
        P("dp", "tensor"),
        P("dp", "tensor"),
        P("dp", "tensor"),
        P("tensor", "dp"),
        P("tensor", None),
        P("tensor", None),
        P("dp", None),
        P(),
    )
    out_specs = P("dp", "tensor", None)
    return jax.shard_map(shards, mesh=mesh, in_specs=in_specs, out_specs=out_specs, check_vma=False)
```
